32 devices in a mesh: gx: 8 (over z, y), gy: 4 (over x, core).
Axes of the slice: x: 2, y: 2, z: 4, core: 2. Of those that a mesh axis runs over, the one named last changes fastest.
Arguments:
- position: float32 [3, 524288], P(None, ('gx', 'gy')), may hold values from -3 to 295.6
- velocity: float32 [3, 524288], P(None, ('gx', 'gy')), may hold values from -0.6 to 0.6
- mass: float32 [524288], P(('gx', 'gy')), may hold values from 0.01 to 0.04
- smoothing: float32 [524288], P(('gx', 'gy')), may hold values from 0.8 to 1.25
- energy: float32 [524288], P(('gx', 'gy')), may hold values from 0.35 to 5.6
- live_blocks: int32 [32], P(('gx', 'gy')), may hold values from 64 to 128, as said below
- send_list: int32 [32, 6, 12], P(('gx', 'gy')), may hold values from 0 to 23, as said below
- nbr_list: int32 [4096, 8], P(('gx', 'gy')), may hold values from 0 to 199, as said below
- nbr_count: int32 [4096], P(('gx', 'gy')), may hold values from 4 to 8
Outputs:
- density: float32 [524288], P(('gx', 'gy'))
- kick: float32 [3, 524288], P(None, ('gx', 'gy'))
- heating: float32 [524288], P(('gx', 'gy'))
The draws below stay inside these ranges and needn't reach their ends.
Inputs may be any that keep to these rules, and one draw needn't show every extreme that they name: `live_blocks`: the live blocks of a domain are its first ones; some domain has all 128 live and some exactly 64. `send_list`: entries are block indices within the sending domain, all among its first 24 blocks and distinct within one peer list; entry 0 of every list p below 4 is block 0. List p below 4 goes to the domain of fine index p in the same segment, list 4 to the previous segment's domain of the same fine index, list 4 + 1 to the next one's. `nbr_list`: entry 0 of a block's list is the block itself; the others are distinct slots: a live block of the own domain, or a slot 128 + p * 12 + s received from another domain, where p is not the domain's own fine index, p = 4 only if a previous segment exists and p = 5 only if a next one exists.
All inputs are finite; a program needn't handle non-finite values.
Results may differ from the reference program's by a relative error of at most 0.0003.
Values sent between devices are 32-bit elements; how exact they have to be, the bound alone decides.
A program may use at most 64 MiB of HBM per device.

```python
import math
import jax
import jax.numpy as jnp
from jax import lax

BLOCK = 128
B_DEV = 128
S = 12
NB = 8
SEGMENTS = 8
FINE = 4
DOMAINS = 32
PEERS = 6
SLOTS = 200
BLOCKS = 4096
PARTICLES = 524288


CELL_SPACING = 1.6


PARTNER_OFFSET = 0.8


BLOCK_SPACING = 2.0


def live_of(key):
    base_key = jax.random.fold_in(key, 101)
    first_key, second_key = jax.random.split(base_key)
    counts = jax.random.randint(first_key, (DOMAINS,), B_DEV // 2, B_DEV + 1, dtype=jnp.int32)
    chosen = jax.random.randint(second_key, (), 0, DOMAINS, dtype=jnp.int32)
    domain_region = jnp.arange(DOMAINS, dtype=jnp.int32)
    counts = jnp.where(domain_region == chosen, B_DEV, counts)
    counts = jnp.where(domain_region == (chosen + 1) % DOMAINS, B_DEV // 2, counts)
    return counts.astype(jnp.int32)


def draw_live_blocks(key, part):
    return live_of(key)


def draw_send_list(key, part):
    counts = live_of(key)
    base_key = jax.random.fold_in(key, 202)
    width_limit = 2 * S
    raw = jax.random.randint(base_key, (DOMAINS, PEERS, width_limit), 0, 4096, dtype=jnp.int32)
    index_value = jnp.arange(width_limit, dtype=jnp.int32)
    score_values = raw * width_limit + index_value[None, None, :]
    full_table = jnp.argmax(counts == B_DEV).astype(jnp.int32)
    domain_region = jnp.arange(DOMAINS, dtype=jnp.int32)[:, None, None]
    peer_domain = jnp.arange(PEERS, dtype=jnp.int32)[None, :, None]
    extra_score = (domain_region == full_table) & (peer_domain == 0) & (index_value[None, None, :] == width_limit - 1) | (domain_region == full_table) & (peer_domain == 1) & (index_value[None, None, :] == 0)
    score_values = score_values + jnp.where(extra_score, 4096 * width_limit, 0)
    first_block = (peer_domain < FINE) & (index_value[None, None, :] == 0)
    score_values = score_values + jnp.where(first_block, 3 * 4096 * width_limit, 0)
    _, picked = lax.top_k(score_values, S)
    return picked.astype(jnp.int32)


def draw_nbr_count(key, part):
    base_key = jax.random.fold_in(key, 303)
    counts = jax.random.randint(base_key, (BLOCKS,), NB // 2, NB + 1, dtype=jnp.int32)
    counts = counts.at[0].set(NB)
    counts = counts.at[1].set(NB // 2)
    return counts.astype(jnp.int32)


def draw_nbr_list(key, part):
    counts = live_of(key)
    sent = draw_send_list(key, part)
    base_key = jax.random.fold_in(key, 404)
    half_fine = max(FINE // 2, 1)
    domain_region = jnp.arange(DOMAINS, dtype=jnp.int32)
    segment = domain_region // FINE
    fine_index = domain_region % FINE
    src_fine = segment[:, None] * FINE + jnp.arange(FINE, dtype=jnp.int32)[None, :]
    ghost_fine = sent[src_fine, fine_index[:, None]].reshape(DOMAINS, FINE * S)
    ghost_lower = sent[jnp.maximum(domain_region - FINE, 0), FINE + 1]
    ghost_upper = sent[jnp.minimum(domain_region + FINE, DOMAINS - 1), FINE]
    ghost_block = jnp.concatenate([ghost_fine, ghost_lower, ghost_upper], axis=1)
    slot = jnp.arange(SLOTS, dtype=jnp.int32)[None, None, :]
    block = jnp.arange(B_DEV, dtype=jnp.int32)[None, :, None]
    peer_domain = (slot - B_DEV) // S
    seg3 = segment[:, None, None]
    fine3 = fine_index[:, None, None]
    local_ok = (slot < counts[:, None, None]) & (slot != block)
    ghost_ok = (peer_domain < FINE) & (peer_domain != fine3) | (peer_domain == FINE) & (seg3 > 0) | (peer_domain == FINE + 1) & (seg3 < SEGMENTS - 1)
    allowed = jnp.where(slot < B_DEV, local_ok, ghost_ok)
    ghost_index = jnp.clip(slot - B_DEV, 0, PEERS * S - 1)
    source_block = jnp.take_along_axis(jnp.broadcast_to(ghost_block[:, None, :], (DOMAINS, 1, PEERS * S)), jnp.broadcast_to(ghost_index, (1, 1, SLOTS)) * jnp.ones((DOMAINS, 1, 1), jnp.int32), axis=2)
    lateral = jnp.abs(jnp.where(peer_domain < FINE, peer_domain % half_fine - fine3 % half_fine, 0))
    local_near = jnp.abs(slot - block) <= 3
    ghost_near = (jnp.abs(source_block - block) <= 2) & (lateral <= 2)
    near = jnp.where(slot < B_DEV, local_near, ghost_near)
    raw = jax.random.randint(base_key, (DOMAINS, B_DEV, SLOTS), 0, 4096, dtype=jnp.int32)
    score_values = raw * SLOTS + slot + jnp.where(near, 4096 * SLOTS, 0)
    forced = (domain_region[:, None, None] == 0) & (block == 0) & (slot == SLOTS - 1)
    partner = (fine3 + half_fine) % FINE
    partner_slot = (block == 0) & (slot == B_DEV + partner * S)
    forced = forced | partner_slot
    score_values = score_values + jnp.where(forced, 2 * 4096 * SLOTS, 0)
    score_values = jnp.where(allowed, score_values, -1)
    _, picked = lax.top_k(score_values, NB - 1)
    itself = jnp.broadcast_to(jnp.arange(B_DEV, dtype=jnp.int32)[None, :, None], (DOMAINS, B_DEV, 1))
    return jnp.concatenate([itself, picked.astype(jnp.int32)], axis=2).reshape(BLOCKS, NB).astype(jnp.int32)


def draw_position(key, part):
    base_key = jax.random.fold_in(key, 606)
    side_key, along_key = jax.random.split(base_key)
    half_fine = max(FINE // 2, 1)
    block = jnp.arange(BLOCKS, dtype=jnp.int32)
    domain_region = block // B_DEV
    inner = block % B_DEV
    segment = domain_region // FINE
    fine_index = domain_region % FINE
    centre_x = (fine_index % half_fine).astype(jnp.float32) * CELL_SPACING
    centre_y = (2 * segment).astype(jnp.float32) * CELL_SPACING + (fine_index // half_fine).astype(jnp.float32) * PARTNER_OFFSET
    centre_z = inner.astype(jnp.float32) * BLOCK_SPACING
    centre = jnp.stack([centre_x, centre_y, centre_z])
    sideways = jnp.clip(0.7 * jax.random.normal(side_key, (2, BLOCKS, BLOCK), jnp.float32), -2.1, 2.1)
    along = jnp.clip(jax.random.normal(along_key, (1, BLOCKS, BLOCK), jnp.float32), -3.0, 3.0)
    spread = jnp.concatenate([sideways, along], axis=0)
    return (centre[:, :, None] + spread).reshape(3, PARTICLES)


def draw_energy(key, part):
    base_key = jax.random.fold_in(key, 505)
    first_key, second_key = jax.random.split(base_key)
    factor = jnp.exp(jax.random.uniform(first_key, (DOMAINS, 1), jnp.float32, math.log(0.5), math.log(4.0)))
    spread = jnp.exp(jax.random.uniform(second_key, (DOMAINS, B_DEV * BLOCK), jnp.float32, math.log(0.7), math.log(1.4)))
    return (factor * spread).reshape(PARTICLES)


def steps_of(key, shape, cuts, least, high):
    gain = 1.0
    for axis_at, blocks in cuts:
        heights = jax.random.uniform(jax.random.fold_in(jax.random.fold_in(key, 6), axis_at), (blocks,), jnp.float32, least / len(cuts), high / len(cuts))
        gain = gain * jnp.repeat(jnp.exp(heights), shape[axis_at] // blocks).reshape((-1,) + (1,) * (len(shape) - 1 - axis_at))
    return gain


def bell_draw(key, dims, scale, bound, cuts=(), held_as=jnp.bfloat16):
    loudness = steps_of(key, dims, cuts, -0.22, 0.18) if cuts else 1.0
    result = jax.random.normal(key, dims, jnp.float32) * scale * loudness
    return jnp.minimum(jnp.maximum(result, -bound), bound).astype(held_as)


def setup_inputs(seed: int = 0) -> dict:
    streams_of = jax.random.split(jax.random.key(seed), 10)
    position = draw_position(jax.random.fold_in(streams_of[9], 71), 0)
    velocity = bell_draw(streams_of[1], (3, PARTICLES), 0.1, 0.6, ((1, 32),), jnp.float32)
    mass = jnp.clip(jnp.exp(math.log(0.04) - 1.3862944 * jax.random.uniform(streams_of[2], (PARTICLES,), jnp.float32) ** steps_of(streams_of[2], (PARTICLES,), ((0, 32),), -0.2, 0.2)), 0.01, 0.04)
    smoothing = jnp.clip(jnp.exp(math.log(1.25) - 0.4462871 * jax.random.uniform(streams_of[3], (PARTICLES,), jnp.float32) ** steps_of(streams_of[3], (PARTICLES,), ((0, 32),), -0.2, 0.2)), 0.8, 1.25)
    energy = draw_energy(jax.random.fold_in(streams_of[9], 71), 0)
    live_blocks = draw_live_blocks(jax.random.fold_in(streams_of[9], 71), 0)
    send_list = draw_send_list(jax.random.fold_in(streams_of[9], 71), 0)
    nbr_list = draw_nbr_list(jax.random.fold_in(streams_of[9], 71), 0)
    nbr_count = draw_nbr_count(jax.random.fold_in(streams_of[9], 71), 0)
    return dict(position=position, velocity=velocity, mass=mass, smoothing=smoothing, energy=energy, live_blocks=live_blocks, send_list=send_list, nbr_list=nbr_list, nbr_count=nbr_count)


GAMMA = 5.0 / 3.0
VISC_ALPHA = 1.0
VISC_BETA = 2.0
ETA_SQUARED = 0.01
COURANT = 0.3
KERNEL_NORM = 21.0 / (16.0 * math.pi)
FAR_STEP = 1e+30

def kernel_sum(target_pos, target_smooth, source_pos, source_weight):
    squares = sum(((target_pos[component][:, None, :] - source_pos[component][:, :, None]) ** 2 for component in range(3)))
    ratio = jnp.sqrt(squares) / target_smooth[:, None, :]
    taper = jnp.maximum(1.0 - 0.5 * ratio, 0.0)
    profile = taper ** 4 * (1.0 + 2.0 * ratio)
    total = lax.optimization_barrier(jnp.sum(source_weight[:, :, None] * profile, axis=1))
    return KERNEL_NORM / target_smooth ** 3 * total

def pressure_terms(dens, thermal):
    return ((GAMMA - 1.0) * thermal / dens, jnp.sqrt(GAMMA * (GAMMA - 1.0) * thermal))

def force_sum(target, source, source_weight, source_valid):
    target_pos, target_vel, target_smooth, target_dens, target_press, target_sound = target
    source_pos, source_vel, source_smooth, source_dens, source_press, source_sound = source
    offsets = [target_pos[component][:, None, :] - source_pos[component][:, :, None] for component in range(3)]
    moving = [target_vel[component][:, None, :] - source_vel[component][:, :, None] for component in range(3)]
    squares = offsets[0] * offsets[0] + offsets[1] * offsets[1] + offsets[2] * offsets[2]
    closing = offsets[0] * moving[0] + offsets[1] * moving[1] + offsets[2] * moving[2]
    mean_smooth = 0.5 * (target_smooth[:, None, :] + source_smooth[:, :, None])
    taper = jnp.maximum(1.0 - 0.5 * jnp.sqrt(squares) / mean_smooth, 0.0)
    slope = -5.0 * KERNEL_NORM * taper ** 3 / mean_smooth ** 5
    approach = mean_smooth * jnp.minimum(closing, 0.0) / (squares + ETA_SQUARED * mean_smooth * mean_smooth)
    mean_sound = 0.5 * (target_sound[:, None, :] + source_sound[:, :, None])
    mean_dens = 0.5 * (target_dens[:, None, :] + source_dens[:, :, None])
    visc = (-VISC_ALPHA * mean_sound * approach + VISC_BETA * approach * approach) / mean_dens
    coef = source_weight[:, :, None] * (target_press[:, None, :] + source_press[:, :, None] + visc) * slope
    accel = jnp.stack([-lax.optimization_barrier(jnp.sum(coef * offset, axis=1)) for offset in offsets])
    rate = 0.5 * lax.optimization_barrier(jnp.sum(coef * closing, axis=1))
    signal = lax.optimization_barrier(jnp.max(jnp.where(source_valid[:, :, None], -approach, 0.0), axis=1))
    return (accel, rate, signal)

def reference(position, velocity, mass, smoothing, energy, live_blocks, send_list, nbr_list, nbr_count):
    domain_region = jnp.arange(DOMAINS, dtype=jnp.int32)
    segment = domain_region // FINE
    fine_index = domain_region % FINE
    peer_ids = jnp.arange(FINE, dtype=jnp.int32)
    src_fine = segment[:, None] * FINE + peer_ids[None, :]
    gid_fine = (src_fine[:, :, None] * B_DEV + send_list[src_fine, fine_index[:, None]]).reshape(DOMAINS, FINE * S)
    src_lower = jnp.maximum(domain_region - FINE, 0)
    gid_lower = src_lower[:, None] * B_DEV + send_list[src_lower, FINE + 1]
    src_upper = jnp.minimum(domain_region + FINE, DOMAINS - 1)
    gid_upper = src_upper[:, None] * B_DEV + send_list[src_upper, FINE]
    gid_own = domain_region[:, None] * B_DEV + jnp.arange(B_DEV, dtype=jnp.int32)[None, :]
    slot_block = jnp.concatenate([gid_own, gid_fine, gid_lower, gid_upper], axis=1).astype(jnp.int32)
    lists = nbr_list.reshape(DOMAINS, B_DEV, NB)
    counts = nbr_count.reshape(DOMAINS, B_DEV)
    usable = jnp.arange(NB, dtype=jnp.int32)[None, None, :] < counts[:, :, None]
    usable = jnp.repeat(usable, BLOCK, axis=2)
    places = position.reshape(3, BLOCKS, BLOCK)
    speeds = velocity.reshape(3, BLOCKS, BLOCK)
    masses = mass.reshape(BLOCKS, BLOCK)
    smooth = smoothing.reshape(BLOCKS, BLOCK)
    thermal = energy.reshape(BLOCKS, BLOCK)

    def density_of(index_value):
        chosen = slot_block[index_value][lists[index_value]]
        source_pos = places[:, chosen].reshape(3, B_DEV, NB * BLOCK)
        weight = jnp.where(usable[index_value], masses[chosen].reshape(B_DEV, NB * BLOCK), 0.0)
        start = (index_value * B_DEV).astype(jnp.int32)
        target_pos = lax.dynamic_slice_in_dim(places, start, B_DEV, 1)
        target_smooth = lax.dynamic_slice_in_dim(smooth, start, B_DEV, 0)
        return kernel_sum(target_pos, target_smooth, source_pos, weight)
    rho = lax.map(density_of, domain_region).reshape(BLOCKS, BLOCK)
    press, sound = pressure_terms(rho, thermal)

    def force_of(index_value):
        chosen = slot_block[index_value][lists[index_value]]
        start = (index_value * B_DEV).astype(jnp.int32)

        def pick(table):
            return table[..., chosen, :].reshape(table.shape[:-2] + (B_DEV, NB * BLOCK))

        def own(table):
            return lax.dynamic_slice_in_dim(table, start, B_DEV, table.ndim - 2)
        weight = jnp.where(usable[index_value], pick(masses), 0.0)
        target = (own(places), own(speeds), own(smooth), own(rho), own(press), own(sound))
        source = (pick(places), pick(speeds), pick(smooth), pick(rho), pick(press), pick(sound))
        return force_sum(target, source, weight, usable[index_value])
    accel, rate, signal = lax.map(force_of, domain_region)
    accel = jnp.moveaxis(accel, 1, 0).reshape(3, PARTICLES)
    rate = rate.reshape(PARTICLES)
    signal = signal.reshape(PARTICLES)
    alive = jnp.arange(B_DEV, dtype=jnp.int32)[None, :, None] < live_blocks[:, None, None]
    alive = jnp.broadcast_to(alive, (DOMAINS, B_DEV, BLOCK)).reshape(PARTICLES)
    sound_flat = sound.reshape(PARTICLES)
    step = COURANT * smoothing / (sound_flat + 1.2 * (VISC_ALPHA * sound_flat + VISC_BETA * signal))
    timestep = jnp.min(jnp.where(alive, step, FAR_STEP))
    density = jnp.where(alive, rho.reshape(PARTICLES), 0.0)
    kick = jnp.where(alive[None, :], timestep * accel, 0.0)
    heating = jnp.where(alive, timestep * rate, 0.0)
    return (density, kick, heating)
```

```python
import functools
import math

import jax
import jax.numpy as jnp
from jax import lax
from jax.experimental import pallas as pl
from jax.experimental.pallas import tpu as pltpu
from jax.sharding import PartitionSpec as P

GAMMA = 5.0 / 3.0
COURANT = 0.3
KERNEL_NORM = 21.0 / (16.0 * math.pi)
FORCE_NORM = 160.0 * KERNEL_NORM
FAR_STEP = 1e30
TINY = 1e-30
SURE = 4
ROWS = 8
VMEM_BYTES = 48 * 1024 * 1024
MESH = pl.DeviceIdType.MESH
X, Y, Z, MASS, SMOOTH, VX, VY, VZ, ENERGY, FIELDS = range(10)
RHO, PRESS, SOUND, DERIVED = range(4)


def inverse(value):
    return pltpu.reciprocal(value, approx=True)


def distance(squares):
    return squares * lax.rsqrt(jnp.maximum(squares, TINY))


def on_diagonal(column, first, row):
    lanes = lax.broadcasted_iota(jnp.int32, row.shape, 1)
    sublanes = lax.broadcasted_iota(jnp.int32, row.shape, 0)
    return row + jnp.where(lanes == sublanes + first, column, 0.0)


def for_neighbours(nbr_ref, count_ref, block, width, visit):
    base = block * width
    visit([nbr_ref[base + j] for j in range(SURE)], True)

    def more(j, carry):
        visit([nbr_ref[base + j]], False)
        return carry

    lax.fori_loop(SURE, count_ref[block], more, 0)


def density_kernel(width, nbr_ref, count_ref, live_ref, table_ref, rho_ref, cols, sums):
    size = table_ref.shape[2]
    rho_ref[...] = jnp.zeros_like(rho_ref)

    def target(block, carry):
        own = table_ref[block]
        turned = own.T
        for place, field in enumerate((X, Y, Z)):
            cols[place] = jnp.broadcast_to(turned[:, field : field + 1], (size, size))
        smooth = jnp.broadcast_to(turned[:, SMOOTH : SMOOTH + 1], (size, size))
        cols[3] = 2.0 * smooth
        cols[4] = 2.5 * smooth

        def visit(slots, fresh):
            sources = [
                [table_ref[slot, pl.ds(field, 1), :] for field in (X, Y, Z, MASS)]
                for slot in slots
            ]
            for first in range(0, size, ROWS):
                rows = pl.ds(first, ROWS)
                x, y, z, reach, edge = [cols[place, rows, :] for place in range(5)]
                total = None if fresh else sums[rows, :]
                for sx, sy, sz, mass in sources:
                    dx, dy, dz = x - sx, y - sy, z - sz
                    squares = dx * dx + dy * dy + dz * dz
                    taper = jnp.maximum(reach - distance(squares), 0.0)
                    square = taper * taper
                    term = (square * square) * (mass * (edge - taper))
                    total = term if total is None else total + term
                sums[rows, :] = total

        for_neighbours(nbr_ref, count_ref, block, width, visit)
        row = jnp.zeros((ROWS, size), jnp.float32)
        for first in range(0, size, ROWS):
            row = on_diagonal(
                jnp.sum(sums[pl.ds(first, ROWS), :], axis=1, keepdims=True), first, row
            )
        total = jnp.sum(row, axis=0, keepdims=True)
        smooth = table_ref[block, pl.ds(SMOOTH, 1), :]
        cube = smooth * smooth * smooth
        rho_ref[pl.ds(block, 1), :] = (KERNEL_NORM / 8.0) * total / (cube * cube * smooth * smooth)
        return carry

    lax.fori_loop(0, live_ref[0], target, 0)


def force_kernel(
    width,
    nbr_ref,
    count_ref,
    live_ref,
    table_ref,
    rho_ref,
    accel_ref,
    rate_ref,
    least_ref,
    derived,
    cols,
    sums,
):
    size = table_ref.shape[2]
    slots = table_ref.shape[0]
    accel_ref[...] = jnp.zeros_like(accel_ref)
    rate_ref[...] = jnp.zeros_like(rate_ref)

    def derive(turn, carry):
        start = pl.multiple_of(turn * ROWS, ROWS)
        rho = rho_ref[pl.ds(start, ROWS), :]
        for i in range(ROWS):
            energy = table_ref[start + i, pl.ds(ENERGY, 1), :]
            own = rho[i : i + 1]
            derived[start + i, pl.ds(RHO, 1), :] = own
            derived[start + i, pl.ds(PRESS, 1), :] = (GAMMA - 1.0) * energy / own
            derived[start + i, pl.ds(SOUND, 1), :] = 0.5 * jnp.sqrt(
                GAMMA * (GAMMA - 1.0) * energy
            )
        return carry

    lax.fori_loop(0, slots // ROWS, derive, 0)
    places = [(table_ref, field) for field in (X, Y, Z, VX, VY, VZ, SMOOTH, MASS)]
    places += [(derived, field) for field in (RHO, PRESS, SOUND)]

    def target(block, least):
        turned = table_ref[block].T
        extra = derived[block].T
        count = 0
        for field in (X, Y, Z, VX, VY, VZ, SMOOTH):
            cols[count] = jnp.broadcast_to(turned[:, field : field + 1], (size, size))
            count += 1
        for field in (RHO, PRESS, SOUND):
            cols[count] = jnp.broadcast_to(extra[:, field : field + 1], (size, size))
            count += 1

        def visit(chosen, fresh):
            sources = [
                [ref[slot, pl.ds(field, 1), :] for ref, field in places] for slot in chosen
            ]
            for first in range(0, size, ROWS):
                rows = pl.ds(first, ROWS)
                x, y, z, vx, vy, vz, smooth, dens, press, sound = [
                    cols[place, rows, :] for place in range(10)
                ]
                totals = None if fresh else [sums[i, rows, :] for i in range(5)]
                for sx, sy, sz, svx, svy, svz, ssmooth, mass, sdens, spress, ssound in sources:
                    dx, dy, dz = x - sx, y - sy, z - sz
                    squares = dx * dx + dy * dy + dz * dz
                    closing = dx * (vx - svx) + dy * (vy - svy) + dz * (vz - svz)
                    reach = smooth + ssmooth
                    reach2 = reach * reach
                    reach4 = reach2 * reach2
                    approach = (
                        reach * jnp.minimum(closing, 0.0) * inverse(squares + 0.0025 * reach2)
                    )
                    visc = approach * (approach - (sound + ssound)) * inverse(dens + sdens)
                    taper = jnp.maximum(reach - distance(squares), 0.0)
                    slope = (taper * taper) * (taper * mass) * inverse(reach4 * reach4)
                    coef = (press + spress + visc) * slope
                    terms = [coef * dx, coef * dy, coef * dz, coef * closing]
                    if totals is None:
                        totals = terms + [approach]
                    else:
                        totals = [a + b for a, b in zip(totals, terms)] + [
                            jnp.minimum(totals[4], approach)
                        ]
                for i in range(5):
                    sums[i, rows, :] = totals[i]

        for_neighbours(nbr_ref, count_ref, block, width, visit)
        lines = [jnp.zeros((ROWS, size), jnp.float32) for _ in range(5)]
        for first in range(0, size, ROWS):
            rows = pl.ds(first, ROWS)
            for i in range(5):
                pick = jnp.sum if i < 4 else jnp.min
                lines[i] = on_diagonal(pick(sums[i, rows, :], axis=1, keepdims=True), first, lines[i])
        lines = [jnp.sum(line, axis=0, keepdims=True) for line in lines]
        for i in range(3):
            accel_ref[i, pl.ds(block, 1), :] = FORCE_NORM * lines[i]
        rate_ref[pl.ds(block, 1), :] = (-0.5 * FORCE_NORM) * lines[3]
        signal = -0.5 * lines[4]
        sound = 2.0 * derived[block, pl.ds(SOUND, 1), :]
        smooth = table_ref[block, pl.ds(SMOOTH, 1), :]
        step = COURANT * smooth / (sound + 1.2 * (sound + 2.0 * signal))
        return jnp.minimum(least, step)

    least = lax.fori_loop(0, live_ref[0], target, jnp.full((1, size), FAR_STEP, jnp.float32))
    least_ref[...] = jnp.broadcast_to(jnp.min(least, axis=1, keepdims=True), least_ref.shape)


def least_kernel(axes, local_ref, out_ref, held, *slots_sems):
    barrier = pltpu.get_barrier_semaphore()
    peers = 0
    for axis, count in axes:
        me = lax.axis_index(axis)
        for step in range(1, count):
            pl.semaphore_signal(
                barrier, inc=1, device_id={axis: lax.rem(me + step, count)}, device_id_type=MESH
            )
        peers += count - 1
    pl.semaphore_wait(barrier, peers)
    held[...] = local_ref[...]
    for i, (axis, count) in enumerate(axes):
        slots, send, recv = slots_sems[3 * i : 3 * i + 3]
        me = lax.axis_index(axis)
        copies = []
        for step in range(1, count):
            copy = pltpu.make_async_remote_copy(
                src_ref=held,
                dst_ref=slots.at[step],
                send_sem=send.at[step],
                recv_sem=recv.at[step],
                device_id={axis: lax.rem(me + step, count)},
                device_id_type=MESH,
            )
            copy.start()
            copies.append(copy)
        for copy in copies:
            copy.wait()
        value = held[...]
        for step in range(1, count):
            value = jnp.minimum(value, slots[step])
        held[...] = value
    out_ref[...] = held[...]


def least_of_all(local, axes):
    scratch = [pltpu.VMEM(local.shape, local.dtype)]
    for _, count in axes:
        scratch += [
            pltpu.VMEM((count,) + local.shape, local.dtype),
            pltpu.SemaphoreType.DMA((count,)),
            pltpu.SemaphoreType.DMA((count,)),
        ]
    return pl.pallas_call(
        functools.partial(least_kernel, axes),
        out_shape=jax.ShapeDtypeStruct(local.shape, local.dtype),
        in_specs=[pl.BlockSpec(memory_space=pltpu.VMEM)],
        out_specs=pl.BlockSpec(memory_space=pltpu.VMEM),
        scratch_shapes=scratch,
        compiler_params=pltpu.CompilerParams(collective_id=0, has_side_effects=True),
        name="least_of_all",
    )(local)


def spread(blocks, send_list, peer_count, slot_count):
    size = lax.axis_size("gx")
    up = [(i, i + 1) for i in range(size - 1)]
    down = [(i + 1, i) for i in range(size - 1)]
    to_fine = send_list[0, :peer_count].reshape(-1)
    outgoing = blocks[to_fine].reshape((peer_count, slot_count) + blocks.shape[1:])
    arrived = lax.all_to_all(outgoing, "gy", split_axis=0, concat_axis=0, tiled=True)
    before = lax.ppermute(blocks[send_list[0, peer_count + 1]], "gx", up)
    after = lax.ppermute(blocks[send_list[0, peer_count]], "gx", down)
    return [arrived.reshape((-1,) + blocks.shape[1:]), before, after]


def shards(
    position, velocity, mass, smoothing, energy, live_blocks, send_list, nbr_list, nbr_count
):
    nx, ny = lax.axis_size("gx"), lax.axis_size("gy")
    block_count = nbr_count.shape[0]
    size = mass.shape[0] // block_count
    slot_count = send_list.shape[2]
    width = nbr_list.shape[1]
    cut = lambda array: array.reshape(block_count, size)
    own = jnp.stack(
        [cut(position[i]) for i in range(3)]
        + [cut(mass), cut(smoothing)]
        + [cut(velocity[i]) for i in range(3)]
        + [cut(energy)],
        axis=1,
    )
    table = jnp.concatenate([own] + spread(own, send_list, ny, slot_count), axis=0)
    slots = table.shape[0]
    lists = nbr_list.reshape(-1)
    smem = pl.BlockSpec(memory_space=pltpu.SMEM)
    vmem = pl.BlockSpec(memory_space=pltpu.VMEM)
    params = pltpu.CompilerParams(vmem_limit_bytes=VMEM_BYTES)
    square = jax.ShapeDtypeStruct((block_count, size), jnp.float32)
    rho = pl.pallas_call(
        functools.partial(density_kernel, width),
        out_shape=square,
        in_specs=[smem, smem, smem, vmem],
        out_specs=vmem,
        scratch_shapes=[
            pltpu.VMEM((5, size, size), jnp.float32),
            pltpu.VMEM((size, size), jnp.float32),
        ],
        compiler_params=params,
        name="density",
    )(lists, nbr_count, live_blocks, table)
    wide_rho = jnp.concatenate([rho] + spread(rho, send_list, ny, slot_count), axis=0)
    accel, rate, least = pl.pallas_call(
        functools.partial(force_kernel, width),
        out_shape=[
            jax.ShapeDtypeStruct((3, block_count, size), jnp.float32),
            square,
            jax.ShapeDtypeStruct((8, 128), jnp.float32),
        ],
        in_specs=[smem, smem, smem, vmem, vmem],
        out_specs=[vmem, vmem, vmem],
        scratch_shapes=[
            pltpu.VMEM((slots, 8, size), jnp.float32),
            pltpu.VMEM((10, size, size), jnp.float32),
            pltpu.VMEM((5, size, size), jnp.float32),
        ],
        compiler_params=params,
        name="force",
    )(lists, nbr_count, live_blocks, table, wide_rho)
    timestep = least_of_all(least, (("gy", ny), ("gx", nx)))[0, 0]
    return (rho.reshape(-1), (timestep * accel).reshape(3, -1), (timestep * rate).reshape(-1))


def solution(mesh):
    return jax.shard_map(
        shards,
        mesh=mesh,
        in_specs=(
            P(None, ("gx", "gy")),
            P(None, ("gx", "gy")),
            P(("gx", "gy")),
            P(("gx", "gy")),
            P(("gx", "gy")),
            P(("gx", "gy")),
            P(("gx", "gy"), None, None),
            P(("gx", "gy"), None),
            P(("gx", "gy")),
        ),
        out_specs=(P(("gx", "gy")), P(None, ("gx", "gy")), P(("gx", "gy"))),
        check_vma=False,
    )
```

```python
import functools
import math

import jax
import jax.numpy as jnp
from jax import lax
from jax.experimental import pallas as pl
from jax.experimental.pallas import tpu as pltpu
from jax.sharding import PartitionSpec as P

GAMMA = 5.0 / 3.0
COURANT = 0.3
KERNEL_NORM = 21.0 / (16.0 * math.pi)
FORCE_NORM = 160.0 * KERNEL_NORM
FAR_STEP = 1e30
TINY = 1e-30
SURE = 4
ROWS = 8
VMEM_BYTES = 48 * 1024 * 1024
MESH = pl.DeviceIdType.MESH
X, Y, Z, MASS, SMOOTH, VX, VY, VZ, ENERGY = range(9)
RHO, PRESS, SOUND = range(8, 11)
OWN_FIELDS = (X, Y, Z, VX, VY, VZ, SMOOTH, RHO, PRESS, SOUND)


def inverse(value):
    return pltpu.reciprocal(value, approx=True)


def distance(squares):
    return squares * lax.rsqrt(jnp.maximum(squares, TINY))


def on_diagonal(column, first, row):
    lanes = lax.broadcasted_iota(jnp.int32, row.shape, 1)
    sublanes = lax.broadcasted_iota(jnp.int32, row.shape, 0)
    return row + jnp.where(lanes == sublanes + first, column, 0.0)


def sweep(width, nbr_ref, count_ref, live_ref, prepare, first_pass, more_pass):
    live = live_ref[0]
    prepare(0)

    def turn(i, carry):
        block = jnp.minimum(i, live - 1)
        after = jnp.minimum(i + 1, live - 1)
        prior = jnp.maximum(i - 1, 0)
        base = block * width
        count = count_ref[block]
        odd = lax.rem(count - SURE, 2)
        for extra in range(2):

            @pl.when(odd == extra)
            def _():
                first_pass([nbr_ref[base + j] for j in range(SURE + extra)], prior)
                prepare(after)

        done = SURE + odd

        def more(j, carry):
            at = base + done + 2 * j
            more_pass([nbr_ref[at], nbr_ref[at + 1]])
            return carry

        return lax.fori_loop(0, (count - done) // 2, more, carry)

    lax.fori_loop(0, live + 1, turn, 0)


def density_kernel(width, nbr_ref, count_ref, live_ref, table_ref, rho_ref, turned, cols, sums):
    size = table_ref.shape[2]
    rho_ref[...] = jnp.zeros_like(rho_ref)
    chunks = [pl.ds(first, ROWS) for first in range(0, size, ROWS)]

    def prepare(block):
        turned[...] = table_ref[block].T

    def read(slots):
        return [
            [table_ref[slot, pl.ds(field, 1), :] for field in (X, Y, Z, MASS)] for slot in slots
        ]

    def summed(columns, sources, total):
        x, y, z, reach, edge = columns
        for sx, sy, sz, mass in sources:
            dx, dy, dz = x - sx, y - sy, z - sz
            squares = dx * dx + dy * dy + dz * dz
            taper = jnp.maximum(reach - distance(squares), 0.0)
            square = taper * taper
            term = (square * square) * (mass * (edge - taper))
            total = term if total is None else total + term
        return total

    def first_pass(slots, prior):
        sources = read(slots)
        line = jnp.zeros((ROWS, size), jnp.float32)
        for rows in chunks:
            line = on_diagonal(jnp.sum(sums[rows, :], axis=1, keepdims=True), rows.start, line)
            own = turned[rows, :]
            columns = [
                jnp.broadcast_to(own[:, field : field + 1], (ROWS, size))
                for field in (X, Y, Z, SMOOTH)
            ]
            columns[3:] = [2.0 * columns[3], 2.5 * columns[3]]
            for i, column in enumerate(columns):
                cols[i, rows, :] = column
            sums[rows, :] = summed(columns, sources, None)
        total = jnp.sum(line, axis=0, keepdims=True)
        smooth = table_ref[prior, pl.ds(SMOOTH, 1), :]
        cube = smooth * smooth * smooth
        rho_ref[pl.ds(prior, 1), :] = (KERNEL_NORM / 8.0) * total / (cube * cube * smooth * smooth)

    def more_pass(slots):
        sources = read(slots)
        for rows in chunks:
            columns = [cols[i, rows, :] for i in range(5)]
            sums[rows, :] = summed(columns, sources, sums[rows, :])

    sweep(width, nbr_ref, count_ref, live_ref, prepare, first_pass, more_pass)


def force_kernel(
    width,
    nbr_ref,
    count_ref,
    live_ref,
    table_ref,
    rho_ref,
    accel_ref,
    rate_ref,
    least_ref,
    full,
    turned,
    cols,
    sums,
):
    size = table_ref.shape[2]
    slots = table_ref.shape[0]
    accel_ref[...] = jnp.zeros_like(accel_ref)
    rate_ref[...] = jnp.zeros_like(rate_ref)
    least_ref[...] = jnp.full(least_ref.shape, FAR_STEP, jnp.float32)
    chunks = [pl.ds(first, ROWS) for first in range(0, size, ROWS)]

    def derive(turn, carry):
        start = pl.multiple_of(turn * ROWS, ROWS)
        rho = rho_ref[pl.ds(start, ROWS), :]
        for i in range(ROWS):
            slot = start + i
            energy = table_ref[slot, pl.ds(ENERGY, 1), :]
            own = rho[i : i + 1]
            full[slot, pl.ds(0, ENERGY), :] = table_ref[slot, pl.ds(0, ENERGY), :]
            full[slot, pl.ds(RHO, 1), :] = own
            full[slot, pl.ds(PRESS, 1), :] = (GAMMA - 1.0) * energy / own
            full[slot, pl.ds(SOUND, 1), :] = 0.5 * jnp.sqrt(GAMMA * (GAMMA - 1.0) * energy)
        return carry

    lax.fori_loop(0, slots // ROWS, derive, 0)

    def prepare(block):
        turned[...] = full[block].T

    def read(chosen):
        return [
            [full[slot, pl.ds(field, 1), :] for field in OWN_FIELDS + (MASS,)] for slot in chosen
        ]

    def summed(columns, sources, totals):
        x, y, z, vx, vy, vz, smooth, dens, press, sound = columns
        for sx, sy, sz, svx, svy, svz, ssmooth, sdens, spress, ssound, mass in sources:
            dx, dy, dz = x - sx, y - sy, z - sz
            squares = dx * dx + dy * dy + dz * dz
            closing = dx * (vx - svx) + dy * (vy - svy) + dz * (vz - svz)
            reach = smooth + ssmooth
            reach2 = reach * reach
            reach4 = reach2 * reach2
            approach = reach * jnp.minimum(closing, 0.0) * inverse(squares + 0.0025 * reach2)
            visc = approach * (approach - (sound + ssound)) * inverse(dens + sdens)
            taper = jnp.maximum(reach - distance(squares), 0.0)
            slope = (taper * taper) * (taper * mass) * inverse(reach4 * reach4)
            coef = (press + spress + visc) * slope
            terms = [coef * dx, coef * dy, coef * dz, coef * closing]
            if totals is None:
                totals = terms + [approach]
            else:
                totals = [a + b for a, b in zip(totals, terms)] + [
                    jnp.minimum(totals[4], approach)
                ]
        return totals

    def first_pass(chosen, prior):
        sources = read(chosen)
        lines = [jnp.zeros((ROWS, size), jnp.float32) for _ in range(5)]
        for rows in chunks:
            for i in range(5):
                pick = jnp.sum if i < 4 else jnp.min
                lines[i] = on_diagonal(
                    pick(sums[i, rows, :], axis=1, keepdims=True), rows.start, lines[i]
                )
            own = turned[rows, :]
            columns = [
                jnp.broadcast_to(own[:, field : field + 1], (ROWS, size)) for field in OWN_FIELDS
            ]
            for i, column in enumerate(columns):
                cols[i, rows, :] = column
            for i, total in enumerate(summed(columns, sources, None)):
                sums[i, rows, :] = total
        lines = [jnp.sum(line, axis=0, keepdims=True) for line in lines]
        for i in range(3):
            accel_ref[i, pl.ds(prior, 1), :] = FORCE_NORM * lines[i]
        rate_ref[pl.ds(prior, 1), :] = (-0.5 * FORCE_NORM) * lines[3]
        signal = -0.5 * lines[4]
        sound = 2.0 * full[prior, pl.ds(SOUND, 1), :]
        smooth = full[prior, pl.ds(SMOOTH, 1), :]
        step = COURANT * smooth / (sound + 1.2 * (sound + 2.0 * signal))
        least_ref[...] = jnp.minimum(least_ref[...], step)

    def more_pass(chosen):
        sources = read(chosen)
        for rows in chunks:
            columns = [cols[i, rows, :] for i in range(len(OWN_FIELDS))]
            totals = [sums[i, rows, :] for i in range(5)]
            for i, total in enumerate(summed(columns, sources, totals)):
                sums[i, rows, :] = total

    sums[...] = jnp.zeros_like(sums)
    sweep(width, nbr_ref, count_ref, live_ref, prepare, first_pass, more_pass)
    least = jnp.min(least_ref[...], axis=1, keepdims=True)
    least_ref[...] = jnp.broadcast_to(least, least_ref.shape)


def least_kernel(axes, local_ref, out_ref, held, *slots_sems):
    barrier = pltpu.get_barrier_semaphore()
    peers = 0
    for axis, count in axes:
        me = lax.axis_index(axis)
        for step in range(1, count):
            pl.semaphore_signal(
                barrier, inc=1, device_id={axis: lax.rem(me + step, count)}, device_id_type=MESH
            )
        peers += count - 1
    pl.semaphore_wait(barrier, peers)
    held[...] = local_ref[...]
    for i, (axis, count) in enumerate(axes):
        slots, send, recv = slots_sems[3 * i : 3 * i + 3]
        me = lax.axis_index(axis)
        copies = []
        for step in range(1, count):
            copy = pltpu.make_async_remote_copy(
                src_ref=held,
                dst_ref=slots.at[step],
                send_sem=send.at[step],
                recv_sem=recv.at[step],
                device_id={axis: lax.rem(me + step, count)},
                device_id_type=MESH,
            )
            copy.start()
            copies.append(copy)
        for copy in copies:
            copy.wait()
        value = held[...]
        for step in range(1, count):
            value = jnp.minimum(value, slots[step])
        held[...] = value
    out_ref[...] = held[...]


def least_of_all(local, axes):
    scratch = [pltpu.VMEM(local.shape, local.dtype)]
    for _, count in axes:
        scratch += [
            pltpu.VMEM((count,) + local.shape, local.dtype),
            pltpu.SemaphoreType.DMA((count,)),
            pltpu.SemaphoreType.DMA((count,)),
        ]
    return pl.pallas_call(
        functools.partial(least_kernel, axes),
        out_shape=jax.ShapeDtypeStruct(local.shape, local.dtype),
        in_specs=[pl.BlockSpec(memory_space=pltpu.VMEM)],
        out_specs=pl.BlockSpec(memory_space=pltpu.VMEM),
        scratch_shapes=scratch,
        compiler_params=pltpu.CompilerParams(collective_id=0, has_side_effects=True),
        name="least_of_all",
    )(local)


def spread(blocks, send_list, peer_count, slot_count):
    size = lax.axis_size("gx")
    up = [(i, i + 1) for i in range(size - 1)]
    down = [(i + 1, i) for i in range(size - 1)]
    to_fine = send_list[0, :peer_count].reshape(-1)
    outgoing = blocks[to_fine].reshape((peer_count, slot_count) + blocks.shape[1:])
    arrived = lax.all_to_all(outgoing, "gy", split_axis=0, concat_axis=0, tiled=True)
    before = lax.ppermute(blocks[send_list[0, peer_count + 1]], "gx", up)
    after = lax.ppermute(blocks[send_list[0, peer_count]], "gx", down)
    return [arrived.reshape((-1,) + blocks.shape[1:]), before, after]


def shards(
    position, velocity, mass, smoothing, energy, live_blocks, send_list, nbr_list, nbr_count
):
    nx, ny = lax.axis_size("gx"), lax.axis_size("gy")
    block_count = nbr_count.shape[0]
    size = mass.shape[0] // block_count
    slot_count = send_list.shape[2]
    width = nbr_list.shape[1]
    cut = lambda array: array.reshape(block_count, size)
    own = jnp.stack(
        [cut(position[i]) for i in range(3)]
        + [cut(mass), cut(smoothing)]
        + [cut(velocity[i]) for i in range(3)]
        + [cut(energy)],
        axis=1,
    )
    table = jnp.concatenate([own] + spread(own, send_list, ny, slot_count), axis=0)
    slots = table.shape[0]
    lists = nbr_list.reshape(-1)
    smem = pl.BlockSpec(memory_space=pltpu.SMEM)
    vmem = pl.BlockSpec(memory_space=pltpu.VMEM)
    params = pltpu.CompilerParams(vmem_limit_bytes=VMEM_BYTES)
    square = jax.ShapeDtypeStruct((block_count, size), jnp.float32)
    rho = pl.pallas_call(
        functools.partial(density_kernel, width),
        out_shape=square,
        in_specs=[smem, smem, smem, vmem],
        out_specs=vmem,
        scratch_shapes=[
            pltpu.VMEM((size, table.shape[1]), jnp.float32),
            pltpu.VMEM((5, size, size), jnp.float32),
            pltpu.VMEM((size, size), jnp.float32),
        ],
        compiler_params=params,
        name="density",
    )(lists, nbr_count, live_blocks, table)
    wide_rho = jnp.concatenate([rho] + spread(rho, send_list, ny, slot_count), axis=0)
    accel, rate, least = pl.pallas_call(
        functools.partial(force_kernel, width),
        out_shape=[
            jax.ShapeDtypeStruct((3, block_count, size), jnp.float32),
            square,
            jax.ShapeDtypeStruct((8, 128), jnp.float32),
        ],
        in_specs=[smem, smem, smem, vmem, vmem],
        out_specs=[vmem, vmem, vmem],
        scratch_shapes=[
            pltpu.VMEM((slots, 16, size), jnp.float32),
            pltpu.VMEM((size, 16), jnp.float32),
            pltpu.VMEM((len(OWN_FIELDS), size, size), jnp.float32),
            pltpu.VMEM((5, size, size), jnp.float32),
        ],
        compiler_params=params,
        name="force",
    )(lists, nbr_count, live_blocks, table, wide_rho)
    timestep = least_of_all(least, (("gy", ny), ("gx", nx)))[0, 0]
    return (rho.reshape(-1), (timestep * accel).reshape(3, -1), (timestep * rate).reshape(-1))


def solution(mesh):
    return jax.shard_map(
        shards,
        mesh=mesh,
        in_specs=(
            P(None, ("gx", "gy")),
            P(None, ("gx", "gy")),
            P(("gx", "gy")),
            P(("gx", "gy")),
            P(("gx", "gy")),
            P(("gx", "gy")),
            P(("gx", "gy"), None, None),
            P(("gx", "gy"), None),
            P(("gx", "gy")),
        ),
        out_specs=(P(("gx", "gy")), P(None, ("gx", "gy")), P(("gx", "gy"))),
        check_vma=False,
    )
```

```python
import functools
import math

import jax
import jax.numpy as jnp
from jax import lax
from jax.experimental import pallas as pl
from jax.experimental.pallas import tpu as pltpu
from jax.sharding import PartitionSpec as P

GAMMA = 5.0 / 3.0
COURANT = 0.3
KERNEL_NORM = 21.0 / (16.0 * math.pi)
FORCE_NORM = 160.0 * KERNEL_NORM
FAR_STEP = 1e30
TINY = 1e-30
SURE = 4
ROWS = 8
VMEM_BYTES = 48 * 1024 * 1024
MESH = pl.DeviceIdType.MESH
X, Y, Z, MASS, SMOOTH, VX, VY, VZ, ENERGY = range(9)
RHO, PRESS, SOUND = range(8, 11)
OWN_FIELDS = (X, Y, Z, VX, VY, VZ, SMOOTH, RHO, PRESS, SOUND)


def inverse(value):
    return pltpu.reciprocal(value, approx=True)


def distance(squares):
    return squares * lax.rsqrt(jnp.maximum(squares, TINY))


def on_diagonal(column, first, row):
    lanes = lax.broadcasted_iota(jnp.int32, row.shape, 1)
    sublanes = lax.broadcasted_iota(jnp.int32, row.shape, 0)
    return row + jnp.where(lanes == sublanes + first, column, 0.0)


def sweep(width, nbr_ref, count_ref, live_ref, prepare, first_pass, more_pass):
    live = live_ref[0]
    prepare(0)

    def turn(i, carry):
        block = jnp.minimum(i, live - 1)
        after = jnp.minimum(i + 1, live - 1)
        prior = jnp.maximum(i - 1, 0)
        base = block * width
        count = count_ref[block]
        odd = lax.rem(count - SURE, 2)
        for extra in range(2):

            @pl.when(odd == extra)
            def _():
                first_pass([nbr_ref[base + j] for j in range(SURE + extra)], prior)
                prepare(after)

        done = SURE + odd

        def more(j, carry):
            at = base + done + 2 * j
            more_pass([nbr_ref[at], nbr_ref[at + 1]])
            return carry

        return lax.fori_loop(0, (count - done) // 2, more, carry)

    lax.fori_loop(0, live + 1, turn, 0)


def grouped(size, count):
    chunks = [pl.ds(first, ROWS) for first in range(0, size, ROWS)]
    return [chunks[i : i + count] for i in range(0, len(chunks), count)]


def density_kernel(
    width, nbr_ref, count_ref, live_ref, table_ref, rho_ref, wide, turned, cols, sums
):
    size = table_ref.shape[2]
    rho_ref[...] = jnp.zeros_like(rho_ref)

    def widen(slot, carry):
        for i, field in enumerate((X, Y, Z, MASS)):
            wide[slot, i] = jnp.broadcast_to(table_ref[slot, pl.ds(field, 1), :], (ROWS, size))
        return carry

    lax.fori_loop(0, table_ref.shape[0], widen, 0)

    def prepare(block):
        turned[...] = table_ref[block].T

    def term(columns, source):
        x, y, z, reach, edge = columns
        sx, sy, sz, mass = source
        dx, dy, dz = x - sx, y - sy, z - sz
        squares = dx * dx + dy * dy + dz * dz
        taper = jnp.maximum(reach - distance(squares), 0.0)
        square = taper * taper
        return (square * square) * (mass * (edge - taper))

    def summed(columns, slots, totals):
        for slot in slots:
            source = [wide[slot, i] for i in range(4)]
            terms = [term(own, source) for own in columns]
            totals = terms if totals is None else [a + b for a, b in zip(totals, terms)]
        return totals

    def first_pass(slots, prior):
        line = jnp.zeros((ROWS, size), jnp.float32)
        for group in grouped(size, 4):
            columns = []
            for rows in group:
                line = on_diagonal(jnp.sum(sums[rows, :], axis=1, keepdims=True), rows.start, line)
                own = turned[rows, :]
                parts = [
                    jnp.broadcast_to(own[:, field : field + 1], (ROWS, size))
                    for field in (X, Y, Z, SMOOTH)
                ]
                parts[3:] = [2.0 * parts[3], 2.5 * parts[3]]
                for i, part in enumerate(parts):
                    cols[i, rows, :] = part
                columns.append(parts)
            for rows, total in zip(group, summed(columns, slots, None)):
                sums[rows, :] = total
        total = jnp.sum(line, axis=0, keepdims=True)
        smooth = table_ref[prior, pl.ds(SMOOTH, 1), :]
        cube = smooth * smooth * smooth
        rho_ref[pl.ds(prior, 1), :] = (KERNEL_NORM / 8.0) * total / (cube * cube * smooth * smooth)

    def more_pass(slots):
        for group in grouped(size, 4):
            columns = [[cols[i, rows, :] for i in range(5)] for rows in group]
            totals = [sums[rows, :] for rows in group]
            for rows, total in zip(group, summed(columns, slots, totals)):
                sums[rows, :] = total

    sweep(width, nbr_ref, count_ref, live_ref, prepare, first_pass, more_pass)


def force_kernel(
    width,
    nbr_ref,
    count_ref,
    live_ref,
    table_ref,
    rho_ref,
    accel_ref,
    rate_ref,
    least_ref,
    full,
    wide,
    turned,
    cols,
    sums,
):
    size = table_ref.shape[2]
    slots = table_ref.shape[0]
    accel_ref[...] = jnp.zeros_like(accel_ref)
    rate_ref[...] = jnp.zeros_like(rate_ref)
    least_ref[...] = jnp.full(least_ref.shape, FAR_STEP, jnp.float32)

    def derive(turn, carry):
        start = pl.multiple_of(turn * ROWS, ROWS)
        rho = rho_ref[pl.ds(start, ROWS), :]
        for i in range(ROWS):
            slot = start + i
            energy = table_ref[slot, pl.ds(ENERGY, 1), :]
            own = rho[i : i + 1]
            full[slot, pl.ds(0, ENERGY), :] = table_ref[slot, pl.ds(0, ENERGY), :]
            full[slot, pl.ds(RHO, 1), :] = own
            full[slot, pl.ds(PRESS, 1), :] = (GAMMA - 1.0) * energy / own
            full[slot, pl.ds(SOUND, 1), :] = 0.5 * jnp.sqrt(GAMMA * (GAMMA - 1.0) * energy)
            for j, field in enumerate(OWN_FIELDS + (MASS,)):
                wide[slot, j] = jnp.broadcast_to(full[slot, pl.ds(field, 1), :], (ROWS, size))
        return carry

    lax.fori_loop(0, slots // ROWS, derive, 0)

    def prepare(block):
        turned[...] = full[block].T

    def terms(columns, source):
        x, y, z, vx, vy, vz, smooth, dens, press, sound = columns
        sx, sy, sz, svx, svy, svz, ssmooth, sdens, spress, ssound, mass = source
        dx, dy, dz = x - sx, y - sy, z - sz
        squares = dx * dx + dy * dy + dz * dz
        closing = dx * (vx - svx) + dy * (vy - svy) + dz * (vz - svz)
        reach = smooth + ssmooth
        reach2 = reach * reach
        reach4 = reach2 * reach2
        approach = reach * jnp.minimum(closing, 0.0) * inverse(squares + 0.0025 * reach2)
        visc = approach * (approach - (sound + ssound)) * inverse(dens + sdens)
        taper = jnp.maximum(reach - distance(squares), 0.0)
        slope = (taper * taper) * (taper * mass) * inverse(reach4 * reach4)
        coef = (press + spress + visc) * slope
        return [coef * dx, coef * dy, coef * dz, coef * closing, approach]

    def joined(totals, more):
        return [a + b for a, b in zip(totals[:4], more)] + [jnp.minimum(totals[4], more[4])]

    def summed(columns, chosen, totals):
        for slot in chosen:
            source = [wide[slot, j] for j in range(len(OWN_FIELDS) + 1)]
            more = [terms(own, source) for own in columns]
            totals = more if totals is None else [joined(*both) for both in zip(totals, more)]
        return totals

    def first_pass(chosen, prior):
        lines = [jnp.zeros((ROWS, size), jnp.float32) for _ in range(5)]
        for group in grouped(size, 2):
            columns = []
            for rows in group:
                for i in range(5):
                    pick = jnp.sum if i < 4 else jnp.min
                    lines[i] = on_diagonal(
                        pick(sums[i, rows, :], axis=1, keepdims=True), rows.start, lines[i]
                    )
                own = turned[rows, :]
                parts = [
                    jnp.broadcast_to(own[:, field : field + 1], (ROWS, size))
                    for field in OWN_FIELDS
                ]
                for i, part in enumerate(parts):
                    cols[i, rows, :] = part
                columns.append(parts)
            for rows, totals in zip(group, summed(columns, chosen, None)):
                for i, total in enumerate(totals):
                    sums[i, rows, :] = total
        lines = [jnp.sum(line, axis=0, keepdims=True) for line in lines]
        for i in range(3):
            accel_ref[i, pl.ds(prior, 1), :] = FORCE_NORM * lines[i]
        rate_ref[pl.ds(prior, 1), :] = (-0.5 * FORCE_NORM) * lines[3]
        signal = -0.5 * lines[4]
        sound = 2.0 * full[prior, pl.ds(SOUND, 1), :]
        smooth = full[prior, pl.ds(SMOOTH, 1), :]
        step = COURANT * smooth / (sound + 1.2 * (sound + 2.0 * signal))
        least_ref[...] = jnp.minimum(least_ref[...], step)

    def more_pass(chosen):
        for group in grouped(size, 2):
            columns = [[cols[i, rows, :] for i in range(len(OWN_FIELDS))] for rows in group]
            totals = [[sums[i, rows, :] for i in range(5)] for rows in group]
            for rows, total in zip(group, summed(columns, chosen, totals)):
                for i in range(5):
                    sums[i, rows, :] = total[i]

    sums[...] = jnp.zeros_like(sums)
    sweep(width, nbr_ref, count_ref, live_ref, prepare, first_pass, more_pass)
    least = jnp.min(least_ref[...], axis=1, keepdims=True)
    least_ref[...] = jnp.broadcast_to(least, least_ref.shape)


def least_kernel(axes, local_ref, out_ref, held, *slots_sems):
    barrier = pltpu.get_barrier_semaphore()
    peers = 0
    for axis, count in axes:
        me = lax.axis_index(axis)
        for step in range(1, count):
            pl.semaphore_signal(
                barrier, inc=1, device_id={axis: lax.rem(me + step, count)}, device_id_type=MESH
            )
        peers += count - 1
    pl.semaphore_wait(barrier, peers)
    held[...] = local_ref[...]
    for i, (axis, count) in enumerate(axes):
        slots, send, recv = slots_sems[3 * i : 3 * i + 3]
        me = lax.axis_index(axis)
        copies = []
        for step in range(1, count):
            copy = pltpu.make_async_remote_copy(
                src_ref=held,
                dst_ref=slots.at[step],
                send_sem=send.at[step],
                recv_sem=recv.at[step],
                device_id={axis: lax.rem(me + step, count)},
                device_id_type=MESH,
            )
            copy.start()
            copies.append(copy)
        for copy in copies:
            copy.wait()
        value = held[...]
        for step in range(1, count):
            value = jnp.minimum(value, slots[step])
        held[...] = value
    out_ref[...] = held[...]


def least_of_all(local, axes):
    scratch = [pltpu.VMEM(local.shape, local.dtype)]
    for _, count in axes:
        scratch += [
            pltpu.VMEM((count,) + local.shape, local.dtype),
            pltpu.SemaphoreType.DMA((count,)),
            pltpu.SemaphoreType.DMA((count,)),
        ]
    return pl.pallas_call(
        functools.partial(least_kernel, axes),
        out_shape=jax.ShapeDtypeStruct(local.shape, local.dtype),
        in_specs=[pl.BlockSpec(memory_space=pltpu.VMEM)],
        out_specs=pl.BlockSpec(memory_space=pltpu.VMEM),
        scratch_shapes=scratch,
        compiler_params=pltpu.CompilerParams(collective_id=0, has_side_effects=True),
        name="least_of_all",
    )(local)


def spread(blocks, send_list, peer_count, slot_count):
    size = lax.axis_size("gx")
    up = [(i, i + 1) for i in range(size - 1)]
    down = [(i + 1, i) for i in range(size - 1)]
    to_fine = send_list[0, :peer_count].reshape(-1)
    outgoing = blocks[to_fine].reshape((peer_count, slot_count) + blocks.shape[1:])
    arrived = lax.all_to_all(outgoing, "gy", split_axis=0, concat_axis=0, tiled=True)
    before = lax.ppermute(blocks[send_list[0, peer_count + 1]], "gx", up)
    after = lax.ppermute(blocks[send_list[0, peer_count]], "gx", down)
    return [arrived.reshape((-1,) + blocks.shape[1:]), before, after]


def shards(
    position, velocity, mass, smoothing, energy, live_blocks, send_list, nbr_list, nbr_count
):
    nx, ny = lax.axis_size("gx"), lax.axis_size("gy")
    block_count = nbr_count.shape[0]
    size = mass.shape[0] // block_count
    slot_count = send_list.shape[2]
    width = nbr_list.shape[1]
    cut = lambda array: array.reshape(block_count, size)
    own = jnp.stack(
        [cut(position[i]) for i in range(3)]
        + [cut(mass), cut(smoothing)]
        + [cut(velocity[i]) for i in range(3)]
        + [cut(energy)],
        axis=1,
    )
    table = jnp.concatenate([own] + spread(own, send_list, ny, slot_count), axis=0)
    slots = table.shape[0]
    lists = nbr_list.reshape(-1)
    smem = pl.BlockSpec(memory_space=pltpu.SMEM)
    vmem = pl.BlockSpec(memory_space=pltpu.VMEM)
    params = pltpu.CompilerParams(vmem_limit_bytes=VMEM_BYTES)
    square = jax.ShapeDtypeStruct((block_count, size), jnp.float32)
    rho = pl.pallas_call(
        functools.partial(density_kernel, width),
        out_shape=square,
        in_specs=[smem, smem, smem, vmem],
        out_specs=vmem,
        scratch_shapes=[
            pltpu.VMEM((slots, 4, ROWS, size), jnp.float32),
            pltpu.VMEM((size, table.shape[1]), jnp.float32),
            pltpu.VMEM((5, size, size), jnp.float32),
            pltpu.VMEM((size, size), jnp.float32),
        ],
        compiler_params=params,
        name="density",
    )(lists, nbr_count, live_blocks, table)
    wide_rho = jnp.concatenate([rho] + spread(rho, send_list, ny, slot_count), axis=0)
    accel, rate, least = pl.pallas_call(
        functools.partial(force_kernel, width),
        out_shape=[
            jax.ShapeDtypeStruct((3, block_count, size), jnp.float32),
            square,
            jax.ShapeDtypeStruct((8, 128), jnp.float32),
        ],
        in_specs=[smem, smem, smem, vmem, vmem],
        out_specs=[vmem, vmem, vmem],
        scratch_shapes=[
            pltpu.VMEM((slots, 16, size), jnp.float32),
            pltpu.VMEM((slots, len(OWN_FIELDS) + 1, ROWS, size), jnp.float32),
            pltpu.VMEM((size, 16), jnp.float32),
            pltpu.VMEM((len(OWN_FIELDS), size, size), jnp.float32),
            pltpu.VMEM((5, size, size), jnp.float32),
        ],
        compiler_params=params,
        name="force",
    )(lists, nbr_count, live_blocks, table, wide_rho)
    timestep = least_of_all(least, (("gy", ny), ("gx", nx)))[0, 0]
    return (rho.reshape(-1), (timestep * accel).reshape(3, -1), (timestep * rate).reshape(-1))


def solution(mesh):
    return jax.shard_map(
        shards,
        mesh=mesh,
        in_specs=(
            P(None, ("gx", "gy")),
            P(None, ("gx", "gy")),
            P(("gx", "gy")),
            P(("gx", "gy")),
            P(("gx", "gy")),
            P(("gx", "gy")),
            P(("gx", "gy"), None, None),
            P(("gx", "gy"), None),
            P(("gx", "gy")),
        ),
        out_specs=(P(("gx", "gy")), P(None, ("gx", "gy")), P(("gx", "gy"))),
        check_vma=False,
    )
```

```python
import functools
import math

import jax
import jax.numpy as jnp
from jax import lax
from jax.experimental import pallas as pl
from jax.experimental.pallas import tpu as pltpu
from jax.sharding import PartitionSpec as P

GAMMA = 5.0 / 3.0
COURANT = 0.3
KERNEL_NORM = 21.0 / (16.0 * math.pi)
FORCE_NORM = 160.0 * KERNEL_NORM
FAR_STEP = 1e30
TINY = 1e-30
SURE = 4
ROWS = 8
VMEM_BYTES = 48 * 1024 * 1024
MESH = pl.DeviceIdType.MESH
X, Y, Z, MASS, SMOOTH, VX, VY, VZ, ENERGY = range(9)
RHO, PRESS, SOUND = range(8, 11)
OWN_FIELDS = (X, Y, Z, VX, VY, VZ, SMOOTH, RHO, PRESS, SOUND)


def inverse(value):
    return pltpu.reciprocal(value, approx=True)


def distance(squares):
    return squares * lax.rsqrt(jnp.maximum(squares, TINY))


def on_diagonal(column, first, row):
    lanes = lax.broadcasted_iota(jnp.int32, row.shape, 1)
    sublanes = lax.broadcasted_iota(jnp.int32, row.shape, 0)
    return row + jnp.where(lanes == sublanes + first, column, 0.0)


def sweep(width, wanted, nbr_ref, count_ref, live_ref, flag_ref, order, steps):
    prepare, head, more_pass, least_done = steps

    def fill(block, n):
        order[n] = block
        return n + jnp.where(flag_ref[block] == wanted, 1, 0)

    chosen = lax.fori_loop(0, live_ref[0], fill, 0)

    def turn(i, carry):
        block = order[jnp.minimum(i, chosen - 1)]
        after = order[jnp.minimum(i + 1, chosen - 1)]
        prior = order[jnp.maximum(i - 1, 0)]
        base = block * width
        count = jnp.where(i < chosen, count_ref[block], 0)
        odd = lax.rem(count, 2)
        if least_done:
            for extra in range(2):

                @pl.when(odd == extra)
                def _():
                    head([nbr_ref[base + j] for j in range(least_done + extra)], prior)
                    prepare(after)

        else:
            head([], prior)
            prepare(after)

            @pl.when(odd == 1)
            def _():
                more_pass([nbr_ref[base]])

        done = least_done + odd

        def more(j, carry):
            at = base + done + 2 * j
            more_pass([nbr_ref[at], nbr_ref[at + 1]])
            return carry

        return lax.fori_loop(0, lax.div(jnp.maximum(count - done, 0), 2), more, carry)

    @pl.when(chosen > 0)
    def _():
        prepare(order[0])
        lax.fori_loop(0, chosen + 1, turn, 0)


def density_kernel(width, wanted, *refs):
    *lists, table_ref = refs[:5]
    rho_ref, order, turned, cols, sums = refs[-5:]
    size = table_ref.shape[2]
    rho_ref[...] = refs[5][...] if wanted else jnp.zeros_like(rho_ref)
    chunks = [pl.ds(first, ROWS) for first in range(0, size, ROWS)]

    def prepare(block):
        turned[...] = table_ref[block].T

    def read(slots):
        return [
            [table_ref[slot, pl.ds(field, 1), :] for field in (X, Y, Z, MASS)] for slot in slots
        ]

    def summed(columns, sources, total):
        x, y, z, reach, edge = columns
        for sx, sy, sz, mass in sources:
            dx, dy, dz = x - sx, y - sy, z - sz
            squares = dx * dx + dy * dy + dz * dz
            taper = jnp.maximum(reach - distance(squares), 0.0)
            square = taper * taper
            term = (square * square) * (mass * (edge - taper))
            total = term if total is None else total + term
        return total

    def first_pass(slots, prior):
        sources = read(slots)
        line = jnp.zeros((ROWS, size), jnp.float32)
        for rows in chunks:
            line = on_diagonal(jnp.sum(sums[rows, :], axis=1, keepdims=True), rows.start, line)
            own = turned[rows, :]
            columns = [
                jnp.broadcast_to(own[:, field : field + 1], (ROWS, size))
                for field in (X, Y, Z, SMOOTH)
            ]
            columns[3:] = [2.0 * columns[3], 2.5 * columns[3]]
            for i, column in enumerate(columns):
                cols[i, rows, :] = column
            sums[rows, :] = summed(columns, sources, None)
        total = jnp.sum(line, axis=0, keepdims=True)
        smooth = table_ref[prior, pl.ds(SMOOTH, 1), :]
        cube = smooth * smooth * smooth
        rho_ref[pl.ds(prior, 1), :] = (KERNEL_NORM / 8.0) * total / (cube * cube * smooth * smooth)

    def more_pass(slots):
        sources = read(slots)
        for rows in chunks:
            columns = [cols[i, rows, :] for i in range(5)]
            sums[rows, :] = summed(columns, sources, sums[rows, :])

    sweep(width, wanted, *lists, order, (prepare, first_pass, more_pass, SURE))


def force_kernel(width, wanted, *refs):
    *lists, table_ref, rho_ref = refs[:6]
    accel_ref, rate_ref, least_ref, order, full, turned, cols, sums = refs[-8:]
    size = table_ref.shape[2]
    slots = table_ref.shape[0]
    if wanted:
        for ref, part in zip((accel_ref, rate_ref, least_ref), refs[6:9]):
            ref[...] = part[...]
    else:
        accel_ref[...] = jnp.zeros_like(accel_ref)
        rate_ref[...] = jnp.zeros_like(rate_ref)
        least_ref[...] = jnp.full(least_ref.shape, FAR_STEP, jnp.float32)
    chunks = [pl.ds(first, ROWS) for first in range(0, size, ROWS)]

    def derive(turn, carry):
        start = pl.multiple_of(turn * ROWS, ROWS)
        rho = rho_ref[pl.ds(start, ROWS), :]
        for i in range(ROWS):
            slot = start + i
            energy = table_ref[slot, pl.ds(ENERGY, 1), :]
            own = rho[i : i + 1]
            full[slot, pl.ds(0, ENERGY), :] = table_ref[slot, pl.ds(0, ENERGY), :]
            full[slot, pl.ds(RHO, 1), :] = own
            full[slot, pl.ds(PRESS, 1), :] = (GAMMA - 1.0) * energy / own
            full[slot, pl.ds(SOUND, 1), :] = 0.5 * jnp.sqrt(GAMMA * (GAMMA - 1.0) * energy)
        return carry

    lax.fori_loop(0, slots // ROWS, derive, 0)

    def prepare(block):
        turned[...] = full[block].T

    def read(chosen):
        return [
            [full[slot, pl.ds(field, 1), :] for field in OWN_FIELDS + (MASS,)] for slot in chosen
        ]

    def summed(columns, sources, totals):
        x, y, z, vx, vy, vz, smooth, dens, press, sound = columns
        for sx, sy, sz, svx, svy, svz, ssmooth, sdens, spress, ssound, mass in sources:
            dx, dy, dz = x - sx, y - sy, z - sz
            squares = dx * dx + dy * dy + dz * dz
            closing = dx * (vx - svx) + dy * (vy - svy) + dz * (vz - svz)
            reach = smooth + ssmooth
            reach2 = reach * reach
            reach4 = reach2 * reach2
            approach = reach * jnp.minimum(closing, 0.0) * inverse(squares + 0.0025 * reach2)
            visc = approach * (approach - (sound + ssound)) * inverse(dens + sdens)
            taper = jnp.maximum(reach - distance(squares), 0.0)
            slope = (taper * taper) * (taper * mass) * inverse(reach4 * reach4)
            coef = (press + spress + visc) * slope
            terms = [coef * dx, coef * dy, coef * dz, coef * closing]
            if totals is None:
                totals = terms + [approach]
            else:
                totals = [a + b for a, b in zip(totals, terms)] + [
                    jnp.minimum(totals[4], approach)
                ]
        return totals

    def first_pass(chosen, prior):
        lines = [jnp.zeros((ROWS, size), jnp.float32) for _ in range(5)]
        for rows in chunks:
            for i in range(5):
                pick = jnp.sum if i < 4 else jnp.min
                lines[i] = on_diagonal(
                    pick(sums[i, rows, :], axis=1, keepdims=True), rows.start, lines[i]
                )
            own = turned[rows, :]
            columns = [
                jnp.broadcast_to(own[:, field : field + 1], (ROWS, size)) for field in OWN_FIELDS
            ]
            for i, column in enumerate(columns):
                cols[i, rows, :] = column
            for i in range(5):
                sums[i, rows, :] = jnp.zeros((ROWS, size), jnp.float32)
        lines = [jnp.sum(line, axis=0, keepdims=True) for line in lines]
        for i in range(3):
            accel_ref[i, pl.ds(prior, 1), :] = FORCE_NORM * lines[i]
        rate_ref[pl.ds(prior, 1), :] = (-0.5 * FORCE_NORM) * lines[3]
        signal = -0.5 * lines[4]
        sound = 2.0 * full[prior, pl.ds(SOUND, 1), :]
        smooth = full[prior, pl.ds(SMOOTH, 1), :]
        step = COURANT * smooth / (sound + 1.2 * (sound + 2.0 * signal))
        least_ref[...] = jnp.minimum(least_ref[...], step)

    def more_pass(chosen):
        sources = read(chosen)
        for rows in chunks:
            columns = [cols[i, rows, :] for i in range(len(OWN_FIELDS))]
            totals = [sums[i, rows, :] for i in range(5)]
            for i, total in enumerate(summed(columns, sources, totals)):
                sums[i, rows, :] = total

    sums[...] = jnp.zeros_like(sums)
    sweep(width, wanted, *lists, order, (prepare, first_pass, more_pass, 0))
    least = jnp.min(least_ref[...], axis=1, keepdims=True)
    least_ref[...] = jnp.broadcast_to(least, least_ref.shape)


def least_kernel(axes, local_ref, out_ref, held, *slots_sems):
    barrier = pltpu.get_barrier_semaphore()
    peers = 0
    for axis, count in axes:
        me = lax.axis_index(axis)
        for step in range(1, count):
            pl.semaphore_signal(
                barrier, inc=1, device_id={axis: lax.rem(me + step, count)}, device_id_type=MESH
            )
        peers += count - 1
    pl.semaphore_wait(barrier, peers)
    held[...] = local_ref[...]
    for i, (axis, count) in enumerate(axes):
        slots, send, recv = slots_sems[3 * i : 3 * i + 3]
        me = lax.axis_index(axis)
        copies = []
        for step in range(1, count):
            copy = pltpu.make_async_remote_copy(
                src_ref=held,
                dst_ref=slots.at[step],
                send_sem=send.at[step],
                recv_sem=recv.at[step],
                device_id={axis: lax.rem(me + step, count)},
                device_id_type=MESH,
            )
            copy.start()
            copies.append(copy)
        for copy in copies:
            copy.wait()
        value = held[...]
        for step in range(1, count):
            value = jnp.minimum(value, slots[step])
        held[...] = value
    out_ref[...] = held[...]


def least_of_all(local, axes):
    scratch = [pltpu.VMEM(local.shape, local.dtype)]
    for _, count in axes:
        scratch += [
            pltpu.VMEM((count,) + local.shape, local.dtype),
            pltpu.SemaphoreType.DMA((count,)),
            pltpu.SemaphoreType.DMA((count,)),
        ]
    return pl.pallas_call(
        functools.partial(least_kernel, axes),
        out_shape=jax.ShapeDtypeStruct(local.shape, local.dtype),
        in_specs=[pl.BlockSpec(memory_space=pltpu.VMEM)],
        out_specs=pl.BlockSpec(memory_space=pltpu.VMEM),
        scratch_shapes=scratch,
        compiler_params=pltpu.CompilerParams(collective_id=0, has_side_effects=True),
        name="least_of_all",
    )(local)


def spread(blocks, send_list, peer_count, slot_count):
    size = lax.axis_size("gx")
    up = [(i, i + 1) for i in range(size - 1)]
    down = [(i + 1, i) for i in range(size - 1)]
    to_fine = send_list[0, :peer_count].reshape(-1)
    outgoing = blocks[to_fine].reshape((peer_count, slot_count) + blocks.shape[1:])
    arrived = lax.all_to_all(outgoing, "gy", split_axis=0, concat_axis=0, tiled=True)
    before = lax.ppermute(blocks[send_list[0, peer_count + 1]], "gx", up)
    after = lax.ppermute(blocks[send_list[0, peer_count]], "gx", down)
    return [arrived.reshape((-1,) + blocks.shape[1:]), before, after]


def shards(
    position, velocity, mass, smoothing, energy, live_blocks, send_list, nbr_list, nbr_count
):
    nx, ny = lax.axis_size("gx"), lax.axis_size("gy")
    block_count = nbr_count.shape[0]
    size = mass.shape[0] // block_count
    slot_count = send_list.shape[2]
    width = nbr_list.shape[1]
    cut = lambda array: array.reshape(block_count, size)
    own = jnp.stack(
        [cut(position[i]) for i in range(3)]
        + [cut(mass), cut(smoothing)]
        + [cut(velocity[i]) for i in range(3)]
        + [cut(energy)],
        axis=1,
    )
    ghosts = spread(own, send_list, ny, slot_count)
    used = jnp.arange(width, dtype=jnp.int32)[None, :] < nbr_count[:, None]
    flags = jnp.any(used & (nbr_list >= block_count), axis=1).astype(jnp.int32)
    lists = (nbr_list.reshape(-1), nbr_count, live_blocks, flags)
    smem = pl.BlockSpec(memory_space=pltpu.SMEM)
    vmem = pl.BlockSpec(memory_space=pltpu.VMEM)
    square = jax.ShapeDtypeStruct((block_count, size), jnp.float32)
    pairs = block_count * width * size * size

    def call(kernel, wanted, name, out, scratch, flops, *operands):
        return pl.pallas_call(
            functools.partial(kernel, width, wanted),
            out_shape=out,
            in_specs=[smem] * len(lists) + [vmem] * len(operands),
            out_specs=jax.tree.map(lambda _: vmem, out),
            scratch_shapes=[pltpu.SMEM((block_count,), jnp.int32)] + scratch,
            compiler_params=pltpu.CompilerParams(vmem_limit_bytes=VMEM_BYTES),
            cost_estimate=pl.CostEstimate(
                flops=flops * pairs, bytes_accessed=4 * own.size, transcendentals=pairs
            ),
            name=name,
        )(*lists, *operands)

    scratch = [
        pltpu.VMEM((size, own.shape[1]), jnp.float32),
        pltpu.VMEM((5, size, size), jnp.float32),
        pltpu.VMEM((size, size), jnp.float32),
    ]
    inner = call(density_kernel, 0, "density_inner", square, scratch, 18, own)
    table = jnp.concatenate([own] + ghosts, axis=0)
    rho = call(density_kernel, 1, "density_edge", square, scratch, 18, table, inner)
    ghosts = spread(rho, send_list, ny, slot_count)
    out = [
        jax.ShapeDtypeStruct((3, block_count, size), jnp.float32),
        square,
        jax.ShapeDtypeStruct((8, 128), jnp.float32),
    ]

    def room(slots):
        return [
            pltpu.VMEM((slots, 16, size), jnp.float32),
            pltpu.VMEM((size, 16), jnp.float32),
            pltpu.VMEM((len(OWN_FIELDS), size, size), jnp.float32),
            pltpu.VMEM((5, size, size), jnp.float32),
        ]

    inner = call(force_kernel, 0, "force_inner", out, room(block_count), 50, own, rho)
    wide_rho = jnp.concatenate([rho] + ghosts, axis=0)
    slots = table.shape[0]
    accel, rate, least = call(
        force_kernel, 1, "force_edge", out, room(slots), 50, table, wide_rho, *inner
    )
    timestep = least_of_all(least, (("gy", ny), ("gx", nx)))[0, 0]
    return (rho.reshape(-1), (timestep * accel).reshape(3, -1), (timestep * rate).reshape(-1))


def solution(mesh):
    return jax.shard_map(
        shards,
        mesh=mesh,
        in_specs=(
            P(None, ("gx", "gy")),
            P(None, ("gx", "gy")),
            P(("gx", "gy")),
            P(("gx", "gy")),
            P(("gx", "gy")),
            P(("gx", "gy")),
            P(("gx", "gy"), None, None),
            P(("gx", "gy"), None),
            P(("gx", "gy")),
        ),
        out_specs=(P(("gx", "gy")), P(None, ("gx", "gy")), P(("gx", "gy"))),
        check_vma=False,
    )
```

```python
import functools
import math

import jax
import jax.numpy as jnp
from jax import lax
from jax.experimental import pallas as pl
from jax.experimental.pallas import tpu as pltpu
from jax.sharding import PartitionSpec as P

GAMMA = 5.0 / 3.0
COURANT = 0.3
KERNEL_NORM = 21.0 / (16.0 * math.pi)
FORCE_NORM = 160.0 * KERNEL_NORM
FAR_STEP = 1e30
TINY = 1e-30
SURE = 4
ROWS = 8
VMEM_BYTES = 48 * 1024 * 1024
MESH = pl.DeviceIdType.MESH
X, Y, Z, MASS, SMOOTH, VX, VY, VZ, ENERGY = range(9)
RHO, PRESS, SOUND = range(8, 11)
OWN_FIELDS = (X, Y, Z, VX, VY, VZ, SMOOTH, RHO, PRESS, SOUND)


def inverse(value):
    return pltpu.reciprocal(value, approx=True)


def distance(squares):
    return squares * lax.rsqrt(jnp.maximum(squares, TINY))


def on_diagonal(column, first, row):
    lanes = lax.broadcasted_iota(jnp.int32, row.shape, 1)
    sublanes = lax.broadcasted_iota(jnp.int32, row.shape, 0)
    return row + jnp.where(lanes == sublanes + first, column, 0.0)


def sweep(width, wanted, nbr_ref, count_ref, live_ref, flag_ref, order, work):
    def fill(block, n):
        order[n] = block
        return n + jnp.where(flag_ref[block] == wanted, 1, 0)

    chosen = lax.fori_loop(0, live_ref[0], fill, 0)

    def turn(i, carry):
        block = order[i]
        count = count_ref[block]
        for n in range(SURE, width + 1):

            @pl.when(count == n)
            def _():
                work(block, [nbr_ref[block * width + j] for j in range(n)])

        return carry

    lax.fori_loop(0, chosen, turn, 0)


def row_sums(size, group, lines, chunk):
    lines = tuple(jnp.zeros((ROWS, size), jnp.float32) for _ in range(lines))

    def part(i, lines):
        for k in range(group):
            first = pl.multiple_of((i * group + k) * ROWS, ROWS)
            values = chunk(pl.ds(first, ROWS))
            lines = tuple(on_diagonal(v, first, line) for v, line in zip(values, lines))
        return lines

    lines = lax.fori_loop(0, size // (ROWS * group), part, lines)
    return [jnp.sum(line, axis=0, keepdims=True) for line in lines]


def lane_sum(value):
    return jnp.sum(value, axis=1, keepdims=True)


def density_kernel(width, wanted, *refs):
    *lists, table_ref = refs[:5]
    rho_ref, order, turned = refs[-3:]
    size = table_ref.shape[2]
    rho_ref[...] = refs[5][...] if wanted else jnp.zeros_like(rho_ref)

    def turn(block, carry):
        turned[block] = table_ref[block].T
        return carry

    lax.fori_loop(0, turned.shape[0], turn, 0, unroll=4)

    def work(block, slots):
        def chunk(rows):
            own = turned[block, rows, :]
            x, y, z, smooth = [
                jnp.broadcast_to(own[:, field : field + 1], (ROWS, size))
                for field in (X, Y, Z, SMOOTH)
            ]
            reach, edge = 2.0 * smooth, 2.5 * smooth
            total = None
            for slot in slots:
                sx, sy, sz, mass = [
                    table_ref[slot, pl.ds(field, 1), :] for field in (X, Y, Z, MASS)
                ]
                dx, dy, dz = x - sx, y - sy, z - sz
                squares = dx * dx + dy * dy + dz * dz
                taper = jnp.maximum(reach - distance(squares), 0.0)
                square = taper * taper
                term = (square * square) * (mass * (edge - taper))
                total = term if total is None else total + term
            return (lane_sum(total),)

        (total,) = row_sums(size, 8, 1, chunk)
        smooth = table_ref[block, pl.ds(SMOOTH, 1), :]
        cube = smooth * smooth * smooth
        rho_ref[pl.ds(block, 1), :] = (KERNEL_NORM / 8.0) * total / (cube * cube * smooth * smooth)

    sweep(width, wanted, *lists, order, work)


def force_kernel(width, wanted, *refs):
    *lists, table_ref, rho_ref = refs[:6]
    accel_ref, rate_ref, least_ref, order, full, turned = refs[-6:]
    size = table_ref.shape[2]
    slots = table_ref.shape[0]
    if wanted:
        for ref, part in zip((accel_ref, rate_ref, least_ref), refs[6:9]):
            ref[...] = part[...]
    else:
        accel_ref[...] = jnp.zeros_like(accel_ref)
        rate_ref[...] = jnp.zeros_like(rate_ref)
        least_ref[...] = jnp.full(least_ref.shape, FAR_STEP, jnp.float32)

    def derive(turn, carry):
        start = pl.multiple_of(turn * ROWS, ROWS)
        rho = rho_ref[pl.ds(start, ROWS), :]
        for i in range(ROWS):
            slot = start + i
            energy = table_ref[slot, pl.ds(ENERGY, 1), :]
            own = rho[i : i + 1]
            full[slot, pl.ds(0, ENERGY), :] = table_ref[slot, pl.ds(0, ENERGY), :]
            full[slot, pl.ds(RHO, 1), :] = own
            full[slot, pl.ds(PRESS, 1), :] = (GAMMA - 1.0) * energy / own
            full[slot, pl.ds(SOUND, 1), :] = 0.5 * jnp.sqrt(GAMMA * (GAMMA - 1.0) * energy)
        return carry

    lax.fori_loop(0, slots // ROWS, derive, 0)

    def turn(block, carry):
        turned[block] = full[block].T
        return carry

    lax.fori_loop(0, turned.shape[0], turn, 0, unroll=4)

    def work(block, chosen):
        def chunk(rows):
            own = turned[block, rows, :]
            x, y, z, vx, vy, vz, smooth, dens, press, sound = [
                jnp.broadcast_to(own[:, field : field + 1], (ROWS, size)) for field in OWN_FIELDS
            ]
            totals = None
            for slot in chosen:
                sx, sy, sz, svx, svy, svz, ssmooth, sdens, spress, ssound, mass = [
                    full[slot, pl.ds(field, 1), :] for field in OWN_FIELDS + (MASS,)
                ]
                dx, dy, dz = x - sx, y - sy, z - sz
                squares = dx * dx + dy * dy + dz * dz
                closing = dx * (vx - svx) + dy * (vy - svy) + dz * (vz - svz)
                reach = smooth + ssmooth
                reach2 = reach * reach
                reach4 = reach2 * reach2
                approach = reach * jnp.minimum(closing, 0.0) * inverse(squares + 0.0025 * reach2)
                visc = approach * (approach - (sound + ssound)) * inverse(dens + sdens)
                taper = jnp.maximum(reach - distance(squares), 0.0)
                slope = (taper * taper) * (taper * mass) * inverse(reach4 * reach4)
                coef = (press + spress + visc) * slope
                terms = [coef * dx, coef * dy, coef * dz, coef * closing]
                if totals is None:
                    totals = terms + [approach]
                else:
                    totals = [a + b for a, b in zip(totals, terms)] + [
                        jnp.minimum(totals[4], approach)
                    ]
            return tuple(lane_sum(total) for total in totals[:4]) + (
                jnp.min(totals[4], axis=1, keepdims=True),
            )

        lines = row_sums(size, 4, 5, chunk)
        for i in range(3):
            accel_ref[i, pl.ds(block, 1), :] = FORCE_NORM * lines[i]
        rate_ref[pl.ds(block, 1), :] = (-0.5 * FORCE_NORM) * lines[3]
        signal = -0.5 * lines[4]
        sound = 2.0 * full[block, pl.ds(SOUND, 1), :]
        smooth = full[block, pl.ds(SMOOTH, 1), :]
        step = COURANT * smooth / (sound + 1.2 * (sound + 2.0 * signal))
        least_ref[...] = jnp.minimum(least_ref[...], step)

    sweep(width, wanted, *lists, order, work)
    least = jnp.min(least_ref[...], axis=1, keepdims=True)
    least_ref[...] = jnp.broadcast_to(least, least_ref.shape)


def least_kernel(axes, local_ref, out_ref, held, *slots_sems):
    barrier = pltpu.get_barrier_semaphore()
    peers = 0
    for axis, count in axes:
        me = lax.axis_index(axis)
        for step in range(1, count):
            pl.semaphore_signal(
                barrier, inc=1, device_id={axis: lax.rem(me + step, count)}, device_id_type=MESH
            )
        peers += count - 1
    pl.semaphore_wait(barrier, peers)
    held[...] = local_ref[...]
    for i, (axis, count) in enumerate(axes):
        slots, send, recv = slots_sems[3 * i : 3 * i + 3]
        me = lax.axis_index(axis)
        copies = []
        for step in range(1, count):
            copy = pltpu.make_async_remote_copy(
                src_ref=held,
                dst_ref=slots.at[step],
                send_sem=send.at[step],
                recv_sem=recv.at[step],
                device_id={axis: lax.rem(me + step, count)},
                device_id_type=MESH,
            )
            copy.start()
            copies.append(copy)
        for copy in copies:
            copy.wait()
        value = held[...]
        for step in range(1, count):
            value = jnp.minimum(value, slots[step])
        held[...] = value
    out_ref[...] = held[...]


def least_of_all(local, axes):
    scratch = [pltpu.VMEM(local.shape, local.dtype)]
    for _, count in axes:
        scratch += [
            pltpu.VMEM((count,) + local.shape, local.dtype),
            pltpu.SemaphoreType.DMA((count,)),
            pltpu.SemaphoreType.DMA((count,)),
        ]
    return pl.pallas_call(
        functools.partial(least_kernel, axes),
        out_shape=jax.ShapeDtypeStruct(local.shape, local.dtype),
        in_specs=[pl.BlockSpec(memory_space=pltpu.VMEM)],
        out_specs=pl.BlockSpec(memory_space=pltpu.VMEM),
        scratch_shapes=scratch,
        compiler_params=pltpu.CompilerParams(collective_id=0, has_side_effects=True),
        name="least_of_all",
    )(local)


def spread(blocks, send_list, peer_count, slot_count):
    size = lax.axis_size("gx")
    up = [(i, i + 1) for i in range(size - 1)]
    down = [(i + 1, i) for i in range(size - 1)]
    to_fine = send_list[0, :peer_count].reshape(-1)
    outgoing = blocks[to_fine].reshape((peer_count, slot_count) + blocks.shape[1:])
    arrived = lax.all_to_all(outgoing, "gy", split_axis=0, concat_axis=0, tiled=True)
    before = lax.ppermute(blocks[send_list[0, peer_count + 1]], "gx", up)
    after = lax.ppermute(blocks[send_list[0, peer_count]], "gx", down)
    return [arrived.reshape((-1,) + blocks.shape[1:]), before, after]


def shards(
    position, velocity, mass, smoothing, energy, live_blocks, send_list, nbr_list, nbr_count
):
    nx, ny = lax.axis_size("gx"), lax.axis_size("gy")
    block_count = nbr_count.shape[0]
    size = mass.shape[0] // block_count
    slot_count = send_list.shape[2]
    width = nbr_list.shape[1]
    cut = lambda array: array.reshape(block_count, size)
    own = jnp.stack(
        [cut(position[i]) for i in range(3)]
        + [cut(mass), cut(smoothing)]
        + [cut(velocity[i]) for i in range(3)]
        + [cut(energy)],
        axis=1,
    )
    ghosts = spread(own, send_list, ny, slot_count)
    used = jnp.arange(width, dtype=jnp.int32)[None, :] < nbr_count[:, None]
    flags = jnp.any(used & (nbr_list >= block_count), axis=1).astype(jnp.int32)
    lists = (nbr_list.reshape(-1), nbr_count, live_blocks, flags)
    smem = pl.BlockSpec(memory_space=pltpu.SMEM)
    vmem = pl.BlockSpec(memory_space=pltpu.VMEM)
    square = jax.ShapeDtypeStruct((block_count, size), jnp.float32)
    pairs = block_count * width * size * size

    def call(kernel, wanted, name, out, scratch, flops, *operands):
        return pl.pallas_call(
            functools.partial(kernel, width, wanted),
            out_shape=out,
            in_specs=[smem] * len(lists) + [vmem] * len(operands),
            out_specs=jax.tree.map(lambda _: vmem, out),
            scratch_shapes=[pltpu.SMEM((block_count,), jnp.int32)] + scratch,
            compiler_params=pltpu.CompilerParams(vmem_limit_bytes=VMEM_BYTES),
            cost_estimate=pl.CostEstimate(
                flops=flops * pairs, bytes_accessed=4 * own.size, transcendentals=pairs
            ),
            name=name,
        )(*lists, *operands)

    scratch = [pltpu.VMEM((block_count, size, own.shape[1]), jnp.float32)]
    inner = call(density_kernel, 0, "density_inner", square, scratch, 18, own)
    table = jnp.concatenate([own] + ghosts, axis=0)
    rho = call(density_kernel, 1, "density_edge", square, scratch, 18, table, inner)
    ghosts = spread(rho, send_list, ny, slot_count)
    out = [
        jax.ShapeDtypeStruct((3, block_count, size), jnp.float32),
        square,
        jax.ShapeDtypeStruct((8, 128), jnp.float32),
    ]

    def room(slots):
        return [
            pltpu.VMEM((slots, 16, size), jnp.float32),
            pltpu.VMEM((block_count, size, 16), jnp.float32),
        ]

    inner = call(force_kernel, 0, "force_inner", out, room(block_count), 50, own, rho)
    wide_rho = jnp.concatenate([rho] + ghosts, axis=0)
    slots = table.shape[0]
    accel, rate, least = call(
        force_kernel, 1, "force_edge", out, room(slots), 50, table, wide_rho, *inner
    )
    timestep = least_of_all(least, (("gy", ny), ("gx", nx)))[0, 0]
    return (rho.reshape(-1), (timestep * accel).reshape(3, -1), (timestep * rate).reshape(-1))


def solution(mesh):
    return jax.shard_map(
        shards,
        mesh=mesh,
        in_specs=(
            P(None, ("gx", "gy")),
            P(None, ("gx", "gy")),
            P(("gx", "gy")),
            P(("gx", "gy")),
            P(("gx", "gy")),
            P(("gx", "gy")),
            P(("gx", "gy"), None, None),
            P(("gx", "gy"), None),
            P(("gx", "gy")),
        ),
        out_specs=(P(("gx", "gy")), P(None, ("gx", "gy")), P(("gx", "gy"))),
        check_vma=False,
    )
```
